32 devices in a mesh: leaf: 16 (over z, x, core), level: 2 (over y).
Axes of the slice: x: 2, y: 2, z: 4, core: 2. Of those that a mesh axis runs over, the one named last changes fastest.
Arguments:
- charges: bfloat16 [384, 128, 256], P(('leaf', 'level')), may hold values from -6 to 6
- near_mat: bfloat16 [384, 16, 128, 128], P(('leaf', 'level')), may hold values from -0.1875 to 0.1875
- near_source: int32 [384, 16], P(('leaf', 'level')), may hold values from 0 to 71
- near_count: int32 [384], P(('leaf', 'level')), may hold values from 1 to 16, as said below
- moment_map: bfloat16 [384, 256, 128], P(('leaf', 'level')), may hold values from -0.109375 to 0.109375
- local_eval: bfloat16 [384, 128, 256], P(('leaf', 'level')), may hold values from -0.375 to 0.375
- upward_child_translation: bfloat16 [8, 256, 256], replicated, may hold values from -0.125 to 0.125
- shift_down: bfloat16 [8, 256, 256], replicated, may hold values from -0.375 to 0.375
- transfer_ops: bfloat16 [8, 256, 256], replicated, may hold values from -0.0625 to 0.0625
- subtree_interaction_list: int32 [16, 32], P('leaf'), may hold values from 0 to 15
- subtree_interaction_operators: int32 [16, 32], P('leaf'), may hold values from 0 to 7
- parent_list: int32 [16, 8], P('leaf'), may hold values from 0 to 1
- parent_ops: int32 [16, 8], P('leaf'), may hold values from 0 to 7
Outputs:
- potential: float32 [384, 128, 256], P(('leaf', 'level'))
The draws below stay inside these ranges and needn't reach their ends.
Inputs may be any that keep to these rules, and one draw needn't show every extreme that they name: `near_count`: some block uses all 16 slots and some block only one.
All inputs are finite; a program needn't handle non-finite values.
Results may differ from the reference program's by a relative error of at most 0.012.
Values may be sent and summed in bfloat16 or wider, within the bound.
A program may use at most 128 MiB of HBM per device.

```python
import jax
import jax.numpy as jnp
from jax import lax

P_SIZE = 128
C = 256
R = 256
NEAR = 16
K0 = 32
K1 = 8
NOPS = 8
SUB = 24
NBLK = 384
LEAVES = 16
PARENTS = 2


def draw_near_count(key, part):
    values = jax.random.randint(key, (NBLK,), 1, NEAR + 1)
    values = values.at[0].set(NEAR)
    values = values.at[1].set(1)
    return values.astype(jnp.int32)


def place_ends(entries, own_key, smallest, largest):
    longest = entries.shape.index(max(entries.shape))
    spots = []
    for shift in (0, 1):
        where = [jax.random.randint(jax.random.fold_in(own_key, axis), (), 0, length) for axis, length in enumerate(entries.shape)]
        where[longest] = (where[longest] + shift) % entries.shape[longest]
        spots.append(tuple(where))
    return entries.at[spots[0]].set(smallest).at[spots[1]].set(largest)


def block_scale(rng, extent, cuts, least, largest):
    loudness = 1.0
    for axis_at, shards_of in cuts:
        heights = jax.random.uniform(jax.random.fold_in(jax.random.fold_in(rng, 6), axis_at), (shards_of,), jnp.float32, least / len(cuts), largest / len(cuts))
        loudness = loudness * jnp.repeat(jnp.exp(heights), extent[axis_at] // shards_of).reshape((-1,) + (1,) * (len(extent) - 1 - axis_at))
    return loudness


def noise(rng, shape, deviation, reach, cuts=(), kind=jnp.bfloat16):
    loudness = block_scale(rng, shape, cuts, -0.22, 0.18) if cuts else 1.0
    array = jax.random.normal(rng, shape, jnp.float32) * deviation * loudness
    return jnp.minimum(jnp.maximum(array, -reach), reach).astype(kind)


def setup_inputs(seed: int = 0) -> dict:
    arg_keys = jax.random.split(jax.random.key(seed), 14)
    charges = noise(arg_keys[0], (NBLK, P_SIZE, R), 1.0, 6.0, ((0, 32),))
    near_mat = noise(arg_keys[1], (NBLK, NEAR, P_SIZE, P_SIZE), (P_SIZE * NEAR // 2) ** -0.5, 0.1875, ((0, 32),))
    near_source = place_ends(jax.random.randint(arg_keys[2], (NBLK, NEAR), 0, 3 * SUB), jax.random.fold_in(arg_keys[2], 1), 0, (3 * SUB) - 1).astype(jnp.int32)
    near_count = draw_near_count(jax.random.fold_in(arg_keys[13], 71), 0)
    moment_map = noise(arg_keys[4], (NBLK, C, P_SIZE), (P_SIZE * SUB) ** -0.5, 0.109375, ((0, 32),))
    local_eval = noise(arg_keys[5], (NBLK, P_SIZE, C), C ** -0.5, 0.375, ((0, 32),))
    upward_child_translation = noise(arg_keys[6], (8, C, C), (8 * C) ** -0.5, 0.125)
    shift_down = noise(arg_keys[7], (8, C, C), C ** -0.5, 0.375)
    transfer_ops = noise(arg_keys[8], (NOPS, C, C), (C * K0) ** -0.5, 0.0625)
    subtree_interaction_list = place_ends(jax.random.randint(arg_keys[9], (LEAVES, K0), 0, LEAVES), jax.random.fold_in(arg_keys[9], 1), 0, LEAVES - 1).astype(jnp.int32)
    subtree_interaction_operators = place_ends(jax.random.randint(arg_keys[10], (LEAVES, K0), 0, NOPS), jax.random.fold_in(arg_keys[10], 1), 0, NOPS - 1).astype(jnp.int32)
    parent_list = place_ends(jax.random.randint(arg_keys[11], (LEAVES, K1), 0, PARENTS), jax.random.fold_in(arg_keys[11], 1), 0, PARENTS - 1).astype(jnp.int32)
    parent_ops = place_ends(jax.random.randint(arg_keys[12], (LEAVES, K1), 0, NOPS), jax.random.fold_in(arg_keys[12], 1), 0, NOPS - 1).astype(jnp.int32)
    return {"charges": charges, "near_mat": near_mat, "near_source": near_source, "near_count": near_count, "moment_map": moment_map, "local_eval": local_eval, "upward_child_translation": upward_child_translation, "shift_down": shift_down, "transfer_ops": transfer_ops, "subtree_interaction_list": subtree_interaction_list, "subtree_interaction_operators": subtree_interaction_operators, "parent_list": parent_list, "parent_ops": parent_ops}


def reference(charges, near_mat, near_source, near_count, moment_map, local_eval, upward_child_translation, shift_down, transfer_ops, subtree_interaction_list, subtree_interaction_operators, parent_list, parent_ops):
    single_precision = jnp.float32
    zero_padding_rows = jnp.zeros((SUB, P_SIZE, R), jnp.bfloat16)
    padded = jnp.concatenate([zero_padding_rows, charges, zero_padding_rows], 0)
    mats = near_mat.reshape(LEAVES, SUB, NEAR, P_SIZE, P_SIZE)
    sources = near_source.reshape(LEAVES, SUB, NEAR)
    counts = near_count.reshape(LEAVES, SUB)

    def near_one(piece_collection):
        block_mat, block_src, block_cnt, leaf_index = piece_collection
        window = lax.dynamic_slice_in_dim(padded, (leaf_index * SUB).astype(jnp.int32), 3 * SUB, 0)
        picked = window[block_src].astype(single_precision)
        active = (jnp.arange(NEAR, dtype=jnp.int32)[None, :] < block_cnt[:, None]).astype(single_precision)
        picked = picked * active[:, :, None, None]
        return jnp.einsum('bkpq,bkqr->bpr', block_mat.astype(single_precision), picked)

    near_part = lax.map(near_one, (mats, sources, counts, jnp.arange(LEAVES, dtype=jnp.int32)))

    def moment_one(piece_collection):
        maps, block_charges = piece_collection
        return jnp.einsum('bcp,bpr->cr', maps.astype(single_precision), block_charges.astype(single_precision)).astype(jnp.bfloat16)

    moments = lax.map(moment_one, (moment_map.reshape(LEAVES, SUB, C, P_SIZE), charges.reshape(LEAVES, SUB, P_SIZE, R)))
    grouped_terms = moments.reshape(PARENTS, 8, C, R)
    upper_levels = jnp.einsum('get,kgtv->kev', upward_child_translation.astype(single_precision), grouped_terms.astype(single_precision)).astype(jnp.bfloat16)

    def local_one(piece_collection):
        leaf_ids, leaf_kinds, parent_ids, parent_kinds, leaf_index = piece_collection
        far_leaf = jnp.einsum('kcd,kdr->cr', transfer_ops[leaf_kinds].astype(single_precision), moments[leaf_ids].astype(single_precision))
        coarse = jnp.einsum('kcd,kdr->cr', transfer_ops[parent_kinds].astype(single_precision), upper_levels[parent_ids].astype(single_precision)).astype(jnp.bfloat16)
        downward = jnp.dot(shift_down[leaf_index % 8], coarse, preferred_element_type=jnp.float32)
        return (far_leaf + downward).astype(jnp.bfloat16)

    local = lax.map(local_one, (subtree_interaction_list, subtree_interaction_operators, parent_list, parent_ops, jnp.arange(LEAVES, dtype=jnp.int32)))

    def far_one(piece_collection):
        evals, expansion = piece_collection
        return jnp.einsum('bpc,cr->bpr', evals.astype(single_precision), expansion.astype(single_precision))

    far_part = lax.map(far_one, (local_eval.reshape(LEAVES, SUB, P_SIZE, C), local))
    return (near_part + far_part).reshape(NBLK, P_SIZE, R)
```

```python
import functools

import jax
import jax.numpy as jnp
from jax import lax
from jax.experimental import pallas as pl
from jax.experimental.pallas import tpu as pltpu
from jax.sharding import PartitionSpec as P

MESH = pl.DeviceIdType.MESH
F32 = jnp.float32
BF16 = jnp.bfloat16


def dot(a, b):
    return jnp.dot(a, b, preferred_element_type=F32)


class Plan:
    def __init__(self, n, rows):
        self.count = 0

        def take(k=1):
            first = self.count
            self.count += k
            return first

        self.own_y = [take(n) for _ in range(2)]
        self.own_x = [take() for _ in range(2)]
        self.own_s = take()
        self.mate_x = take(n)
        self.mate_s = [take(n) for _ in range(2)]
        self.outer_y = take(n)
        self.part_y = take(n)
        self.cell_x = take()
        self.cell_z = take(rows)
        self.cell_s = take()
        self.local_y = take(n)


def kernel(
    leaves,
    n,
    plan,
    sources,
    counts,
    cell_list,
    cell_ops,
    up_list,
    up_ops,
    charges,
    near_mat,
    moment_map,
    local_eval,
    upward,
    shift,
    transfer,
    out,
    ext,
    near_v,
    map_v,
    eval_v,
    upward_v,
    shift_v,
    transfer_v,
    part_f,
    part_b,
    part_in,
    every,
    upper,
    local,
    load_sem,
    send_sem,
    recv_sem,
):
    nb, slots = near_mat.shape[0], near_mat.shape[1]
    half = nb // 2
    sub = n * nb
    coeffs = moment_map.shape[1]
    width = part_b.shape[2]
    rows = leaves // 4
    parents = leaves // 8

    leaf = lax.axis_index("leaf")
    level = lax.axis_index("level")
    core = lax.rem(leaf, 2)
    at_x = lax.rem(leaf // 2, 2)
    row = leaf // 4
    sibling = leaf + 1 - 2 * core
    across = leaf + 2 - 4 * at_x
    outer = leaf - 1 + 2 * core
    has_outer = jnp.logical_and(outer >= 0, outer < leaves)

    def mate(d):
        return (leaf, lax.rem(level + d, n))

    def from_level(d):
        return lax.rem(level + n - d, n)

    to_sibling = (sibling, level)
    to_outer = (outer, level)
    to_across = (across, level)

    def to_row(e):
        return (lax.rem(row + e, rows) * 4 + lax.rem(leaf, 4), level)

    def blocks(part, lev, h=None):
        start = (part * n + lev) * nb
        if h is None:
            return ext.at[pl.ds(start, nb)]
        return ext.at[pl.ds(start + h * half, half)]

    def remote(src, dst, to, i):
        return pltpu.make_async_remote_copy(
            src_ref=src,
            dst_ref=dst,
            send_sem=send_sem.at[i],
            recv_sem=recv_sem.at[i],
            device_id=to,
            device_id_type=MESH,
        )

    loads = [
        pltpu.make_async_copy(src, dst, load_sem.at[i])
        for i, (src, dst) in enumerate(
            [
                (charges, blocks(1, level)),
                (moment_map, map_v),
                (upward, upward_v),
                (transfer, transfer_v),
                (shift, shift_v),
                (local_eval, eval_v),
                (near_mat, near_v),
            ]
        )
    ]
    for copy in loads:
        copy.start()

    ext[3 * sub] = jnp.zeros(ext.shape[1:], ext.dtype)

    @pl.when(jnp.logical_not(has_outer))
    def _():
        @pl.loop(0, sub)
        def _(i):
            ext[i] = jnp.zeros(ext.shape[1:], ext.dtype)

    barrier = pltpu.get_barrier_semaphore()
    peers = [mate(d) for d in range(1, n)] + [to_sibling, to_across]
    peers += [to_row(e) for e in range(1, rows)]
    for peer in peers:
        pl.semaphore_signal(barrier, inc=1, device_id=peer, device_id_type=MESH)

    @pl.when(has_outer)
    def _():
        pl.semaphore_signal(barrier, inc=1, device_id=to_outer, device_id_type=MESH)

    pl.semaphore_wait(barrier, len(peers) + has_outer.astype(jnp.int32))

    def own_y(d, h):
        return remote(
            charges.at[pl.ds(h * half, half)], blocks(1, level, h), mate(d), plan.own_y[h] + d
        )

    def own_x(h):
        return remote(
            charges.at[pl.ds(h * half, half)], blocks(0, level, h), to_outer, plan.own_x[h]
        )

    def mate_x(d):
        q = from_level(d)
        return remote(blocks(1, q, 0), blocks(0, q, 0), to_outer, plan.mate_x + d)

    def mate_s(d, h):
        q = from_level(d)
        return remote(blocks(1, q, h), blocks(2, q, h), to_sibling, plan.mate_s[h] + d)

    def outer_y(d):
        return remote(blocks(0, level, 1), blocks(0, level, 1), mate(d), plan.outer_y + d)

    own_s = remote(charges, blocks(2, level), to_sibling, plan.own_s)
    mates = range(1, n)

    for d in mates:
        own_y(d, 0).start()

    @pl.when(has_outer)
    def _():
        own_x(1).start()

    own_s.start()

    loads[0].wait()
    loads[1].wait()
    mine = ext[pl.ds((n + level) * nb, nb)].reshape(nb * ext.shape[1], ext.shape[2])
    maps = jnp.concatenate([map_v[b] for b in range(nb)], axis=1)
    partial = dot(maps, mine)
    for j in range(n):
        piece = partial[:, j * width : (j + 1) * width]
        part_f[j] = piece
        part_b[j] = piece.astype(BF16)

    def part_y(d):
        return remote(part_b.at[lax.rem(level + d, n)], part_in.at[d], mate(d), plan.part_y + d)

    for d in mates:
        part_y(d).start()
    for d in mates:
        own_y(d, 1).start()

    total = part_f[level]
    for d in mates:
        part_y(d).wait_recv()
        total = total + part_in[d].astype(F32)
    every[core, row, at_x] = total.astype(BF16)
    cell = every.at[core, row, at_x]
    cell_x = remote(cell, cell, to_across, plan.cell_x)
    cell_x.start()

    @pl.when(has_outer)
    def _():
        own_x(0).start()

    for d in mates:
        own_y(d, 0).wait_recv()

        @pl.when(has_outer)
        def _():
            mate_x(d).start()

        mate_s(d, 0).start()

    cell_x.wait_recv()

    def cell_z(e):
        pair = every.at[core, row]
        return remote(pair, pair, to_row(e), plan.cell_z + e)

    for e in range(1, rows):
        cell_z(e).start()

    @pl.when(has_outer)
    def _():
        own_x(1).wait_recv()
        for d in mates:
            outer_y(d).start()

    for e in range(1, rows):
        cell_z(e).wait_recv()
    cell_s = remote(every.at[core], every.at[core], to_sibling, plan.cell_s)
    cell_s.start()
    for d in mates:
        own_y(d, 1).wait_recv()
        mate_s(d, 1).start()
    cell_s.wait_recv()

    for copy in loads[2:5]:
        copy.wait()

    def cell_of(i):
        return every[lax.rem(i, 2), i // 4, lax.rem(i // 2, 2)]

    @pl.loop(0, parents)
    def _(p):
        acc = jnp.zeros((coeffs, width), F32)
        for i in range(8):
            acc = acc + dot(upward_v[i], cell_of(p * 8 + i))
        upper[p] = acc.astype(BF16)

    coarse = jnp.zeros((coeffs, width), F32)
    for k in range(up_list.shape[1]):
        coarse = coarse + dot(transfer_v[up_ops[0, k]], upper[up_list[0, k]])
    down = dot(shift_v[lax.rem(leaf, 8)], coarse.astype(BF16))

    def far_step(k, acc):
        for j in range(4):
            i = k * 4 + j
            acc = acc + dot(transfer_v[cell_ops[0, i]], cell_of(cell_list[0, i]))
        return acc

    far = lax.fori_loop(0, cell_list.shape[1] // 4, far_step, down)
    local[level] = far.astype(BF16)

    def local_y(d):
        return remote(local.at[level], local.at[level], mate(d), plan.local_y + d)

    for d in mates:
        local_y(d).start()
    loads[5].wait()
    loads[6].wait()

    own_s.wait_recv()
    for d in mates:
        mate_s(d, 0).wait_recv()
        mate_s(d, 1).wait_recv()

    @pl.when(has_outer)
    def _():
        own_x(0).wait_recv()
        for d in mates:
            mate_x(d).wait_recv()
            outer_y(d).wait_recv()

    for d in mates:
        local_y(d).wait_recv()

    expansion = jnp.concatenate([local[j] for j in range(n)], axis=1)

    @pl.loop(0, nb)
    def _(b):
        acc = dot(eval_v[b], expansion)
        picked = []
        for k in range(slots):
            s = sources[b, k]
            part = (s >= sub).astype(jnp.int32) + (s >= 2 * sub).astype(jnp.int32)
            s = s + core * (2 - 2 * part) * sub
            picked.append(ext[jnp.where(k < counts[b], s, 3 * sub)])
        for k in range(0, slots, 2):
            left = jnp.concatenate([near_v[b, k], near_v[b, k + 1]], axis=1)
            acc = acc + dot(left, jnp.concatenate(picked[k : k + 2], axis=0))
        out[b] = acc

    for d in mates:
        own_y(d, 0).wait_send()
        own_y(d, 1).wait_send()
        part_y(d).wait_send()
        mate_s(d, 0).wait_send()
        mate_s(d, 1).wait_send()
        local_y(d).wait_send()
    own_s.wait_send()
    cell_x.wait_send()
    cell_s.wait_send()
    for e in range(1, rows):
        cell_z(e).wait_send()

    @pl.when(has_outer)
    def _():
        own_x(0).wait_send()
        own_x(1).wait_send()
        for d in mates:
            mate_x(d).wait_send()
            outer_y(d).wait_send()


def on_device(
    leaves,
    n,
    charges,
    near_mat,
    near_source,
    near_count,
    moment_map,
    local_eval,
    upward_child_translation,
    shift_down,
    transfer_ops,
    subtree_interaction_list,
    subtree_interaction_operators,
    parent_list,
    parent_ops,
):
    nb, p_size, cols = charges.shape
    coeffs = moment_map.shape[1]
    width = cols // n
    rows = leaves // 4
    plan = Plan(n, rows)
    smem = pl.BlockSpec(memory_space=pltpu.SMEM)
    hbm = pl.BlockSpec(memory_space=pl.ANY)

    def buf(like):
        return pltpu.VMEM(like.shape, like.dtype)

    return pl.pallas_call(
        functools.partial(kernel, leaves, n, plan),
        out_shape=jax.ShapeDtypeStruct((nb, p_size, cols), F32),
        in_specs=[smem] * 6 + [hbm] * 7,
        out_specs=pl.BlockSpec(memory_space=pltpu.VMEM),
        scratch_shapes=[
            pltpu.VMEM((3 * n * nb + 1, p_size, cols), BF16),
            buf(near_mat),
            buf(moment_map),
            buf(local_eval),
            buf(upward_child_translation),
            buf(shift_down),
            buf(transfer_ops),
            pltpu.VMEM((n, coeffs, width), F32),
            pltpu.VMEM((n, coeffs, width), BF16),
            pltpu.VMEM((n, coeffs, width), BF16),
            pltpu.VMEM((2, rows, 2, coeffs, width), BF16),
            pltpu.VMEM((leaves // 8, coeffs, width), BF16),
            pltpu.VMEM((n, coeffs, width), BF16),
            pltpu.SemaphoreType.DMA((7,)),
            pltpu.SemaphoreType.DMA((plan.count,)),
            pltpu.SemaphoreType.DMA((plan.count,)),
        ],
        compiler_params=pltpu.CompilerParams(
            collective_id=0, has_side_effects=True, vmem_limit_bytes=56 * 2**20
        ),
    )(
        near_source,
        near_count,
        subtree_interaction_list,
        subtree_interaction_operators,
        parent_list,
        parent_ops,
        charges,
        near_mat,
        moment_map,
        local_eval,
        upward_child_translation,
        shift_down,
        transfer_ops,
    )


def solution(mesh):
    split = P(("leaf", "level"))
    placed = (split,) * 6 + (P(),) * 3 + (P("leaf"),) * 4
    return jax.shard_map(
        functools.partial(on_device, mesh.shape["leaf"], mesh.shape["level"]),
        mesh=mesh,
        in_specs=placed,
        out_specs=split,
        check_vma=False,
    )
```

```python
import functools

import jax
import jax.numpy as jnp
from jax import lax
from jax.experimental import pallas as pl
from jax.experimental.pallas import tpu as pltpu
from jax.sharding import PartitionSpec as P

MESH = pl.DeviceIdType.MESH
F32 = jnp.float32
BF16 = jnp.bfloat16


def dot(a, b):
    return jnp.dot(a, b, preferred_element_type=F32)


def pieces(nb, by_x, cuts_x, cuts_y):
    def cut(start, stop, cuts):
        at = [start + (stop - start) * i // cuts for i in range(cuts + 1)]
        return [(a, b - a) for a, b in zip(at, at[1:]) if b > a]

    return cut(0, by_x, cuts_x), cut(by_x, nb, cuts_y)


class Plan:
    def __init__(self, n, rows, runs):
        self.count = 0

        def take(k=1):
            first = self.count
            self.count += k
            return first

        self.own_y = {r: take(n) for r in runs}
        self.own_x = {r: take() for r in runs}
        self.own_s = take()
        self.mate_x = {r: take(n) for r in runs}
        self.mate_s = {r: take(n) for r in runs}
        self.outer_y = {r: take(n) for r in runs}
        self.part_y = take(n)
        self.cell_x = take()
        self.cell_z = take(rows)
        self.cell_s = take()
        self.local_y = take(n)


def kernel(
    leaves,
    n,
    plan,
    by_x,
    by_y,
    sources,
    counts,
    cell_list,
    cell_ops,
    up_list,
    up_ops,
    charges,
    near_mat,
    moment_map,
    local_eval,
    upward,
    shift,
    transfer,
    out,
    ext,
    near_v,
    map_v,
    eval_v,
    upward_v,
    shift_v,
    transfer_v,
    part_f,
    part_b,
    part_in,
    every,
    upper,
    local,
    load_sem,
    send_sem,
    recv_sem,
):
    nb, slots = near_mat.shape[0], near_mat.shape[1]
    sub = n * nb
    coeffs = moment_map.shape[1]
    width = part_b.shape[2]
    rows = leaves // 4
    parents = leaves // 8

    leaf = lax.axis_index("leaf")
    level = lax.axis_index("level")
    core = lax.rem(leaf, 2)
    at_x = lax.rem(leaf // 2, 2)
    row = leaf // 4
    sibling = leaf + 1 - 2 * core
    across = leaf + 2 - 4 * at_x
    outer = leaf - 1 + 2 * core
    has_outer = jnp.logical_and(outer >= 0, outer < leaves)

    def mate(d):
        return (leaf, lax.rem(level + d, n))

    def from_level(d):
        return lax.rem(level + n - d, n)

    to_sibling = (sibling, level)
    to_outer = (outer, level)
    to_across = (across, level)

    def to_row(e):
        return (lax.rem(row + e, rows) * 4 + lax.rem(leaf, 4), level)

    def blocks(part, lev, run=None):
        start = (part * n + lev) * nb
        first, length = run or (0, nb)
        return ext.at[pl.ds(start + first, length)]

    def remote(src, dst, to, i):
        return pltpu.make_async_remote_copy(
            src_ref=src,
            dst_ref=dst,
            send_sem=send_sem.at[i],
            recv_sem=recv_sem.at[i],
            device_id=to,
            device_id_type=MESH,
        )

    loads = [
        pltpu.make_async_copy(src, dst, load_sem.at[i])
        for i, (src, dst) in enumerate(
            [
                (charges, blocks(1, level)),
                (moment_map, map_v),
                (upward, upward_v),
                (transfer, transfer_v),
                (shift, shift_v),
                (local_eval, eval_v),
                (near_mat, near_v),
            ]
        )
    ]
    for copy in loads:
        copy.start()

    ext[3 * sub] = jnp.zeros(ext.shape[1:], ext.dtype)

    @pl.when(jnp.logical_not(has_outer))
    def _():
        @pl.loop(0, sub)
        def _(i):
            ext[i] = jnp.zeros(ext.shape[1:], ext.dtype)

    barrier = pltpu.get_barrier_semaphore()
    peers = [mate(d) for d in range(1, n)] + [to_sibling, to_across]
    peers += [to_row(e) for e in range(1, rows)]
    for peer in peers:
        pl.semaphore_signal(barrier, inc=1, device_id=peer, device_id_type=MESH)

    @pl.when(has_outer)
    def _():
        pl.semaphore_signal(barrier, inc=1, device_id=to_outer, device_id_type=MESH)

    loads[0].wait()
    loads[1].wait()
    mine = ext[pl.ds((n + level) * nb, nb)].reshape(nb * ext.shape[1], ext.shape[2])
    maps = jnp.concatenate([map_v[b] for b in range(nb)], axis=1)
    partial = dot(maps, mine)
    for j in range(n):
        piece = partial[:, j * width : (j + 1) * width]
        part_f[j] = piece
        part_b[j] = piece.astype(BF16)

    pl.semaphore_wait(barrier, len(peers) + has_outer.astype(jnp.int32))

    def own_y(d, run):
        return remote(
            charges.at[pl.ds(*run)], blocks(1, level, run), mate(d), plan.own_y[run] + d
        )

    def own_x(run):
        return remote(charges.at[pl.ds(*run)], blocks(0, level, run), to_outer, plan.own_x[run])

    def mate_x(d, run):
        q = from_level(d)
        return remote(blocks(1, q, run), blocks(0, q, run), to_outer, plan.mate_x[run] + d)

    def mate_s(d, run):
        q = from_level(d)
        return remote(blocks(1, q, run), blocks(2, q, run), to_sibling, plan.mate_s[run] + d)

    def outer_y(d, run):
        return remote(blocks(0, level, run), blocks(0, level, run), mate(d), plan.outer_y[run] + d)

    own_s = remote(charges, blocks(2, level), to_sibling, plan.own_s)
    mates = range(1, n)

    def part_y(d):
        return remote(part_b.at[lax.rem(level + d, n)], part_in.at[d], mate(d), plan.part_y + d)

    def send_y(runs):
        for run in runs:
            for d in mates:
                own_y(d, run).start()

    def send_x(runs):
        @pl.when(has_outer)
        def _():
            for run in runs:
                own_x(run).start()

    for d in mates:
        part_y(d).start()
    send_y(by_x[:1])
    send_x(by_y[:1])
    own_s.start()

    total = part_f[level]
    for d in mates:
        part_y(d).wait_recv()
        total = total + part_in[d].astype(F32)
    every[core, row, at_x] = total.astype(BF16)
    cell = every.at[core, row, at_x]
    cell_x = remote(cell, cell, to_across, plan.cell_x)
    cell_x.start()
    send_y(by_x[1:])
    send_x(by_y[1:])
    cell_x.wait_recv()

    def cell_z(e):
        pair = every.at[core, row]
        return remote(pair, pair, to_row(e), plan.cell_z + e)

    for e in range(1, rows):
        cell_z(e).start()
    send_y(by_y)

    def forward_y(runs):
        @pl.when(has_outer)
        def _():
            for run in runs:
                own_x(run).wait_recv()
                for d in mates:
                    outer_y(d, run).start()

    def forward_x(runs):
        for run in runs:
            for d in mates:
                own_y(d, run).wait_recv()

                @pl.when(has_outer)
                def _():
                    mate_x(d, run).start()

                mate_s(d, run).start()

    send_x(by_x)
    forward_x(by_x)
    forward_y(by_y)

    for e in range(1, rows):
        cell_z(e).wait_recv()
    cell_s = remote(every.at[core], every.at[core], to_sibling, plan.cell_s)
    cell_s.start()
    for run in by_y:
        for d in mates:
            own_y(d, run).wait_recv()
            mate_s(d, run).start()
    cell_s.wait_recv()

    for copy in loads[2:5]:
        copy.wait()

    def cell_of(i):
        return every[lax.rem(i, 2), i // 4, lax.rem(i // 2, 2)]

    @pl.loop(0, parents)
    def _(p):
        acc = jnp.zeros((coeffs, width), F32)
        for i in range(8):
            acc = acc + dot(upward_v[i], cell_of(p * 8 + i))
        upper[p] = acc.astype(BF16)

    coarse = jnp.zeros((coeffs, width), F32)
    for k in range(up_list.shape[1]):
        coarse = coarse + dot(transfer_v[up_ops[0, k]], upper[up_list[0, k]])
    down = dot(shift_v[lax.rem(leaf, 8)], coarse.astype(BF16))

    def far_step(k, acc):
        for j in range(4):
            i = k * 4 + j
            acc = acc + dot(transfer_v[cell_ops[0, i]], cell_of(cell_list[0, i]))
        return acc

    far = lax.fori_loop(0, cell_list.shape[1] // 4, far_step, down)
    local[level] = far.astype(BF16)

    def local_y(d):
        return remote(local.at[level], local.at[level], mate(d), plan.local_y + d)

    for d in mates:
        local_y(d).start()
    loads[5].wait()
    loads[6].wait()

    own_s.wait_recv()
    for run in by_x + by_y:
        for d in mates:
            mate_s(d, run).wait_recv()

    @pl.when(has_outer)
    def _():
        for run in by_x:
            own_x(run).wait_recv()
            for d in mates:
                mate_x(d, run).wait_recv()
        for run in by_y:
            for d in mates:
                outer_y(d, run).wait_recv()

    for d in mates:
        local_y(d).wait_recv()

    expansion = jnp.concatenate([local[j] for j in range(n)], axis=1)

    @pl.loop(0, nb)
    def _(b):
        acc = dot(eval_v[b], expansion)
        picked = []
        for k in range(slots):
            s = sources[b, k]
            part = (s >= sub).astype(jnp.int32) + (s >= 2 * sub).astype(jnp.int32)
            s = s + core * (2 - 2 * part) * sub
            picked.append(ext[jnp.where(k < counts[b], s, 3 * sub)])
        for k in range(0, slots, 2):
            left = jnp.concatenate([near_v[b, k], near_v[b, k + 1]], axis=1)
            acc = acc + dot(left, jnp.concatenate(picked[k : k + 2], axis=0))
        out[b] = acc

    for d in mates:
        part_y(d).wait_send()
        local_y(d).wait_send()
        for run in by_x + by_y:
            own_y(d, run).wait_send()
            mate_s(d, run).wait_send()
    own_s.wait_send()
    cell_x.wait_send()
    cell_s.wait_send()
    for e in range(1, rows):
        cell_z(e).wait_send()

    @pl.when(has_outer)
    def _():
        for run in by_x + by_y:
            own_x(run).wait_send()
        for d in mates:
            for run in by_x:
                mate_x(d, run).wait_send()
            for run in by_y:
                outer_y(d, run).wait_send()


def on_device(
    leaves,
    n,
    charges,
    near_mat,
    near_source,
    near_count,
    moment_map,
    local_eval,
    upward_child_translation,
    shift_down,
    transfer_ops,
    subtree_interaction_list,
    subtree_interaction_operators,
    parent_list,
    parent_ops,
):
    nb, p_size, cols = charges.shape
    coeffs = moment_map.shape[1]
    width = cols // n
    rows = leaves // 4
    by_x, by_y = pieces(nb, nb // 2, 2, 2)
    plan = Plan(n, rows, by_x + by_y)
    smem = pl.BlockSpec(memory_space=pltpu.SMEM)
    hbm = pl.BlockSpec(memory_space=pl.ANY)

    def buf(like):
        return pltpu.VMEM(like.shape, like.dtype)

    return pl.pallas_call(
        functools.partial(kernel, leaves, n, plan, by_x, by_y),
        out_shape=jax.ShapeDtypeStruct((nb, p_size, cols), F32),
        in_specs=[smem] * 6 + [hbm] * 7,
        out_specs=pl.BlockSpec(memory_space=pltpu.VMEM),
        scratch_shapes=[
            pltpu.VMEM((3 * n * nb + 1, p_size, cols), BF16),
            buf(near_mat),
            buf(moment_map),
            buf(local_eval),
            buf(upward_child_translation),
            buf(shift_down),
            buf(transfer_ops),
            pltpu.VMEM((n, coeffs, width), F32),
            pltpu.VMEM((n, coeffs, width), BF16),
            pltpu.VMEM((n, coeffs, width), BF16),
            pltpu.VMEM((2, rows, 2, coeffs, width), BF16),
            pltpu.VMEM((leaves // 8, coeffs, width), BF16),
            pltpu.VMEM((n, coeffs, width), BF16),
            pltpu.SemaphoreType.DMA((7,)),
            pltpu.SemaphoreType.DMA((plan.count,)),
            pltpu.SemaphoreType.DMA((plan.count,)),
        ],
        compiler_params=pltpu.CompilerParams(
            collective_id=0, has_side_effects=True, vmem_limit_bytes=56 * 2**20
        ),
    )(
        near_source,
        near_count,
        subtree_interaction_list,
        subtree_interaction_operators,
        parent_list,
        parent_ops,
        charges,
        near_mat,
        moment_map,
        local_eval,
        upward_child_translation,
        shift_down,
        transfer_ops,
    )


def solution(mesh):
    split = P(("leaf", "level"))
    placed = (split,) * 6 + (P(),) * 3 + (P("leaf"),) * 4
    return jax.shard_map(
        functools.partial(on_device, mesh.shape["leaf"], mesh.shape["level"]),
        mesh=mesh,
        in_specs=placed,
        out_specs=split,
        check_vma=False,
    )
```

```python
import functools

import jax
import jax.numpy as jnp
from jax import lax
from jax.experimental import pallas as pl
from jax.experimental.pallas import tpu as pltpu
from jax.sharding import PartitionSpec as P

MESH = pl.DeviceIdType.MESH
F32 = jnp.float32
BF16 = jnp.bfloat16


def dot(a, b):
    return jnp.dot(a, b, preferred_element_type=F32)


def pieces(nb, by_x, cuts_x, cuts_y):
    def cut(start, stop, cuts):
        at = [start + (stop - start) * i // cuts for i in range(cuts + 1)]
        return [(a, b - a) for a, b in zip(at, at[1:]) if b > a]

    return cut(0, by_x, cuts_x), cut(by_x, nb, cuts_y)


class Plan:
    def __init__(self, n, rows, runs):
        self.count = 0

        def take(k=1):
            first = self.count
            self.count += k
            return first

        self.own_y = {r: take(n) for r in runs}
        self.own_x = {r: take() for r in runs}
        self.own_s = take()
        self.mate_x = {r: take(n) for r in runs}
        self.mate_s = {r: take(n) for r in runs}
        self.outer_y = {r: take(n) for r in runs}
        self.part_y = take(n)
        self.cell_x = take()
        self.cell_z = take(rows)
        self.cell_s = take()
        self.local_y = take(n)


def kernel(
    leaves,
    n,
    plan,
    by_x,
    by_y,
    sources,
    counts,
    cell_list,
    cell_ops,
    up_list,
    up_ops,
    charges,
    near_mat,
    moment_map,
    local_eval,
    upward,
    shift,
    transfer,
    out,
    ext,
    near_v,
    map_v,
    eval_v,
    upward_v,
    shift_v,
    transfer_v,
    part_f,
    part_b,
    part_in,
    every,
    upper,
    local,
    load_sem,
    send_sem,
    recv_sem,
):
    nb, slots = near_mat.shape[0], near_mat.shape[1]
    sub = n * nb
    coeffs = moment_map.shape[1]
    width = part_b.shape[2]
    rows = leaves // 4
    parents = leaves // 8

    leaf = lax.axis_index("leaf")
    level = lax.axis_index("level")
    core = lax.rem(leaf, 2)
    at_x = lax.rem(leaf // 2, 2)
    row = leaf // 4
    sibling = leaf + 1 - 2 * core
    across = leaf + 2 - 4 * at_x
    outer = leaf - 1 + 2 * core
    has_outer = jnp.logical_and(outer >= 0, outer < leaves)

    def mate(d):
        return (leaf, lax.rem(level + d, n))

    def from_level(d):
        return lax.rem(level + n - d, n)

    to_sibling = (sibling, level)
    to_outer = (outer, level)
    to_across = (across, level)

    def to_row(e):
        return (lax.rem(row + e, rows) * 4 + lax.rem(leaf, 4), level)

    def blocks(part, lev, run=None):
        start = (part * n + lev) * nb
        first, length = run or (0, nb)
        return ext.at[pl.ds(start + first, length)]

    def remote(src, dst, to, i):
        return pltpu.make_async_remote_copy(
            src_ref=src,
            dst_ref=dst,
            send_sem=send_sem.at[i],
            recv_sem=recv_sem.at[i],
            device_id=to,
            device_id_type=MESH,
        )

    loads = [
        pltpu.make_async_copy(src, dst, load_sem.at[i])
        for i, (src, dst) in enumerate(
            [
                (charges, blocks(1, level)),
                (moment_map, map_v),
                (upward, upward_v),
                (transfer, transfer_v),
                (shift, shift_v),
                (local_eval, eval_v),
                (near_mat, near_v),
            ]
        )
    ]
    for copy in loads:
        copy.start()

    ext[3 * sub] = jnp.zeros(ext.shape[1:], ext.dtype)

    @pl.when(jnp.logical_not(has_outer))
    def _():
        @pl.loop(0, sub)
        def _(i):
            ext[i] = jnp.zeros(ext.shape[1:], ext.dtype)

    barrier = pltpu.get_barrier_semaphore()
    peers = [mate(d) for d in range(1, n)] + [to_sibling, to_across]
    peers += [to_row(e) for e in range(1, rows)]
    for peer in peers:
        pl.semaphore_signal(barrier, inc=1, device_id=peer, device_id_type=MESH)

    @pl.when(has_outer)
    def _():
        pl.semaphore_signal(barrier, inc=1, device_id=to_outer, device_id_type=MESH)

    loads[0].wait()
    loads[1].wait()
    mine = ext[pl.ds((n + level) * nb, nb)].reshape(nb * ext.shape[1], ext.shape[2])
    maps = jnp.concatenate([map_v[b] for b in range(nb)], axis=1)
    partial = dot(maps, mine)
    for j in range(n):
        piece = partial[:, j * width : (j + 1) * width]
        part_f[j] = piece
        part_b[j] = piece.astype(BF16)

    pl.semaphore_wait(barrier, len(peers) + has_outer.astype(jnp.int32))

    def own_y(d, run):
        return remote(
            charges.at[pl.ds(*run)], blocks(1, level, run), mate(d), plan.own_y[run] + d
        )

    def own_x(run):
        return remote(charges.at[pl.ds(*run)], blocks(0, level, run), to_outer, plan.own_x[run])

    def mate_x(d, run):
        q = from_level(d)
        return remote(blocks(1, q, run), blocks(0, q, run), to_outer, plan.mate_x[run] + d)

    def mate_s(d, run):
        q = from_level(d)
        return remote(blocks(1, q, run), blocks(2, q, run), to_sibling, plan.mate_s[run] + d)

    def outer_y(d, run):
        return remote(blocks(0, level, run), blocks(0, level, run), mate(d), plan.outer_y[run] + d)

    own_s = remote(charges, blocks(2, level), to_sibling, plan.own_s)
    mates = range(1, n)

    def part_y(d):
        return remote(part_b.at[lax.rem(level + d, n)], part_in.at[d], mate(d), plan.part_y + d)

    def send_y(runs):
        for run in runs:
            for d in mates:
                own_y(d, run).start()

    def send_x(runs):
        @pl.when(has_outer)
        def _():
            for run in runs:
                own_x(run).start()

    for d in mates:
        part_y(d).start()
    send_y(by_x[:1])
    send_x(by_y[:1])
    own_s.start()

    total = part_f[level]
    for d in mates:
        part_y(d).wait_recv()
        total = total + part_in[d].astype(F32)
    every[core, row, at_x] = total.astype(BF16)
    cell = every.at[core, row, at_x]
    cell_x = remote(cell, cell, to_across, plan.cell_x)
    cell_x.start()
    send_y(by_x[1:])
    send_x(by_y[1:])
    cell_x.wait_recv()

    def cell_z(e):
        pair = every.at[core, row]
        return remote(pair, pair, to_row(e), plan.cell_z + e)

    for e in range(1, rows):
        cell_z(e).start()
    send_y(by_y)

    def forward_y(runs):
        @pl.when(has_outer)
        def _():
            for run in runs:
                own_x(run).wait_recv()
                for d in mates:
                    outer_y(d, run).start()

    def forward_x(runs):
        for run in runs:
            for d in mates:
                own_y(d, run).wait_recv()

                @pl.when(has_outer)
                def _():
                    mate_x(d, run).start()

                mate_s(d, run).start()

    send_x(by_x)
    forward_x(by_x)
    forward_y(by_y)

    for e in range(1, rows):
        cell_z(e).wait_recv()
    cell_s = remote(every.at[core], every.at[core], to_sibling, plan.cell_s)
    cell_s.start()
    for run in by_y:
        for d in mates:
            own_y(d, run).wait_recv()
            mate_s(d, run).start()
    cell_s.wait_recv()

    for copy in loads[2:5]:
        copy.wait()

    def cell_of(i):
        return every[lax.rem(i, 2), i // 4, lax.rem(i // 2, 2)]

    @pl.loop(0, parents)
    def _(p):
        acc = jnp.zeros((coeffs, width), F32)
        for i in range(8):
            acc = acc + dot(upward_v[i], cell_of(p * 8 + i))
        upper[p] = acc.astype(BF16)

    coarse = jnp.zeros((coeffs, width), F32)
    for k in range(up_list.shape[1]):
        coarse = coarse + dot(transfer_v[up_ops[0, k]], upper[up_list[0, k]])
    down = dot(shift_v[lax.rem(leaf, 8)], coarse.astype(BF16))

    def far_step(k, acc):
        for j in range(4):
            i = k * 4 + j
            acc = acc + dot(transfer_v[cell_ops[0, i]], cell_of(cell_list[0, i]))
        return acc

    far = lax.fori_loop(0, cell_list.shape[1] // 4, far_step, down)
    local[level] = far.astype(BF16)

    def local_y(d):
        return remote(local.at[level], local.at[level], mate(d), plan.local_y + d)

    for d in mates:
        local_y(d).start()
    loads[5].wait()
    loads[6].wait()

    own_s.wait_recv()
    for run in by_x + by_y:
        for d in mates:
            mate_s(d, run).wait_recv()

    @pl.when(has_outer)
    def _():
        for run in by_x:
            own_x(run).wait_recv()
            for d in mates:
                mate_x(d, run).wait_recv()
        for run in by_y:
            for d in mates:
                outer_y(d, run).wait_recv()

    for d in mates:
        local_y(d).wait_recv()

    expansion = jnp.concatenate([local[j] for j in range(n)], axis=1)

    @pl.loop(0, nb)
    def _(b):
        acc = dot(eval_v[b], expansion)
        picked = []
        for k in range(slots):
            s = sources[b, k]
            part = (s >= sub).astype(jnp.int32) + (s >= 2 * sub).astype(jnp.int32)
            s = s + core * (2 - 2 * part) * sub
            picked.append(ext[jnp.where(k < counts[b], s, 3 * sub)])
        for k in range(0, slots, 2):
            left = jnp.concatenate([near_v[b, k], near_v[b, k + 1]], axis=1)
            acc = acc + dot(left, jnp.concatenate(picked[k : k + 2], axis=0))
        out[b] = acc.astype(BF16)

    for d in mates:
        part_y(d).wait_send()
        local_y(d).wait_send()
        for run in by_x + by_y:
            own_y(d, run).wait_send()
            mate_s(d, run).wait_send()
    own_s.wait_send()
    cell_x.wait_send()
    cell_s.wait_send()
    for e in range(1, rows):
        cell_z(e).wait_send()

    @pl.when(has_outer)
    def _():
        for run in by_x + by_y:
            own_x(run).wait_send()
        for d in mates:
            for run in by_x:
                mate_x(d, run).wait_send()
            for run in by_y:
                outer_y(d, run).wait_send()


def on_device(
    leaves,
    n,
    charges,
    near_mat,
    near_source,
    near_count,
    moment_map,
    local_eval,
    upward_child_translation,
    shift_down,
    transfer_ops,
    subtree_interaction_list,
    subtree_interaction_operators,
    parent_list,
    parent_ops,
):
    nb, p_size, cols = charges.shape
    coeffs = moment_map.shape[1]
    width = cols // n
    rows = leaves // 4
    by_x, by_y = pieces(nb, nb // 2, 2, 2)
    plan = Plan(n, rows, by_x + by_y)
    smem = pl.BlockSpec(memory_space=pltpu.SMEM)
    hbm = pl.BlockSpec(memory_space=pl.ANY)

    def buf(like):
        return pltpu.VMEM(like.shape, like.dtype)

    return pl.pallas_call(
        functools.partial(kernel, leaves, n, plan, by_x, by_y),
        out_shape=jax.ShapeDtypeStruct((nb, p_size, cols), BF16),
        in_specs=[smem] * 6 + [hbm] * 7,
        out_specs=pl.BlockSpec(memory_space=pltpu.VMEM),
        scratch_shapes=[
            pltpu.VMEM((3 * n * nb + 1, p_size, cols), BF16),
            buf(near_mat),
            buf(moment_map),
            buf(local_eval),
            buf(upward_child_translation),
            buf(shift_down),
            buf(transfer_ops),
            pltpu.VMEM((n, coeffs, width), F32),
            pltpu.VMEM((n, coeffs, width), BF16),
            pltpu.VMEM((n, coeffs, width), BF16),
            pltpu.VMEM((2, rows, 2, coeffs, width), BF16),
            pltpu.VMEM((leaves // 8, coeffs, width), BF16),
            pltpu.VMEM((n, coeffs, width), BF16),
            pltpu.SemaphoreType.DMA((7,)),
            pltpu.SemaphoreType.DMA((plan.count,)),
            pltpu.SemaphoreType.DMA((plan.count,)),
        ],
        compiler_params=pltpu.CompilerParams(
            collective_id=0, has_side_effects=True, vmem_limit_bytes=56 * 2**20
        ),
    )(
        near_source,
        near_count,
        subtree_interaction_list,
        subtree_interaction_operators,
        parent_list,
        parent_ops,
        charges,
        near_mat,
        moment_map,
        local_eval,
        upward_child_translation,
        shift_down,
        transfer_ops,
    ).astype(F32)


def solution(mesh):
    split = P(("leaf", "level"))
    placed = (split,) * 6 + (P(),) * 3 + (P("leaf"),) * 4
    return jax.shard_map(
        functools.partial(on_device, mesh.shape["leaf"], mesh.shape["level"]),
        mesh=mesh,
        in_specs=placed,
        out_specs=split,
        check_vma=False,
    )
```
